32 devices in a mesh: seq: 8 (over y, x, core), resp: 4 (over z).
Axes of the slice: x: 2, y: 2, z: 4, core: 2. Of those that a mesh axis runs over, the one named last changes fastest.
Arguments:
- prompt_keys: bfloat16 [2, 1024, 512], P(None, 'seq'), may hold values from -6.1 to 6.1
- prompt_values: bfloat16 [2, 1024, 512], P(None, 'seq'), may hold values from -6 to 6
- resp_query: bfloat16 [8, 1024, 4096], P('resp', None, 'seq'), may hold values from -121 to 121
- resp_keys: bfloat16 [8, 1024, 512], P('resp'), may hold values from -6 to 6
- resp_values: bfloat16 [8, 1024, 512], P('resp'), may hold values from -6 to 6
- prompt_x: bfloat16 [2, 1024, 8192], P(None, 'seq', 'resp'), may hold values from -6 to 6
- prompt_dt: float32 [2, 128, 1024], P(None, 'resp', 'seq'), may hold values from 0 to 0.5, as said below
- prompt_b: bfloat16 [2, 1024, 128], P(None, 'seq'), may hold values from -6 to 6
- prompt_c: bfloat16 [2, 1024, 128], P(None, 'seq'), may hold values from -0.5 to 0.5
- resp_x: bfloat16 [8, 1024, 8192], P('resp', None, 'seq'), may hold values from -6 to 6
- resp_dt: float32 [8, 128, 1024], P('resp', 'seq'), may hold values from 0 to 0.5, as said below
- resp_b: bfloat16 [8, 1024, 128], P('resp'), may hold values from -6 to 6
- resp_c: bfloat16 [8, 1024, 128], P('resp'), may hold values from -0.5 to 0.5
- ssm_rate: float32 [128], replicated, may hold values from 0.7 to 1.4
- resp_group: int32 [8], P('resp'), may hold values from 0 to 1
- resp_len: int32 [8], P('resp'), may hold values from 1 to 1024, 5120 in all
Outputs:
- resp_attn_out: bfloat16 [8, 1024, 4096], P('resp', None, 'seq')
- resp_ssm_out: bfloat16 [8, 1024, 8192], P('resp', None, 'seq')
- prompt_ssm_out: bfloat16 [2, 1024, 8192], P(None, 'seq', 'resp')
The draws below stay inside these ranges and needn't reach their ends.
Inputs may be any that keep to these rules, and one draw needn't show every extreme that they name: `prompt_dt`: positive step sizes. `resp_dt`: positive step sizes.
All inputs are finite; a program needn't handle non-finite values. No bound on the sum of `resp_len` on one device may be relied on, other than what follows from the above.
Results may differ from the reference program's by a relative error of at most 0.0048.
Values may be sent and summed in bfloat16 or wider, within the bound.
A program may use at most 192 MiB of HBM per device.

```python
import math
import jax
import jax.numpy as jnp
import numpy as np
from jax import lax

HDIM = 128
QPK = 8
HEADS = 32
KVH = 4
SP = 64
NST = 128
SSM_HEADS = 128
QS = 128
PROMPTS = 2
P_DEV = 128
PLEN = 1024
RESPONSES = 8
RLEN = 1024


def key_table(key):
    table = jax.random.normal(jax.random.fold_in(key, 1), (PROMPTS, PLEN, KVH * HDIM), jnp.float32)
    return jnp.clip(table, -6.0, 6.0)


def draw_prompt_keys(key, part):
    table = key_table(key)
    return table.astype(jnp.bfloat16)


def draw_resp_query(key, part):
    queries = 2.5 * jnp.clip(jax.random.normal(jax.random.fold_in(key, 2), (RESPONSES, RLEN, HEADS * HDIM), jnp.float32), -6.0, 6.0)
    return queries.astype(jnp.bfloat16)


def draw_prompt_x(key, part):
    shards = PLEN // P_DEV
    shape = (PROMPTS, shards, P_DEV, SSM_HEADS, SP)
    base = jnp.clip(jax.random.normal(jax.random.fold_in(key, 41), shape, jnp.float32), -6.0, 6.0)
    loud = jax.random.uniform(jax.random.fold_in(key, 42), (PROMPTS, shards, 1, SSM_HEADS, 1)) < 0.5
    level = jax.random.uniform(jax.random.fold_in(key, 43), (PROMPTS, shards, 1, SSM_HEADS, 1))
    amplitude = jnp.where(loud, jnp.exp(jnp.log(0.5) * level), 0.02 * jnp.exp(jnp.log(1.5) * level))
    return (base * amplitude).reshape(PROMPTS, PLEN, SSM_HEADS * SP).astype(jnp.bfloat16)


def slow_heads(key):
    share = 0.5
    return jax.random.uniform(jax.random.fold_in(key, 21), (SSM_HEADS,)) < share


def change_sizes_abs(key, diagonal_lookup_vector, element_tally, window_extent, packet_clusters):
    span = PLEN + RLEN
    slow = slow_heads(key)
    unit_draw = jax.random.uniform(jax.random.fold_in(diagonal_lookup_vector, 1), (element_tally, SSM_HEADS, 1))
    gradual_rate_floor = jnp.exp(jnp.log(0.05 / span) + unit_draw * jnp.log(6.0))
    fast_base = jnp.exp(jnp.log(0.008) + unit_draw * jnp.log(6.25))
    base_rate = jnp.where(slow[None, :, None], gradual_rate_floor, fast_base)
    rough = jnp.exp(jax.random.uniform(jax.random.fold_in(diagonal_lookup_vector, 2), (element_tally, SSM_HEADS, window_extent), jnp.float32, -0.4, 0.4))
    block_factor = jnp.exp(jax.random.uniform(jax.random.fold_in(diagonal_lookup_vector, 3), (element_tally, SSM_HEADS, window_extent // QS, 1), jnp.float32, jnp.log(0.5), jnp.log(2.0)))
    block_factor = jnp.broadcast_to(block_factor, (element_tally, SSM_HEADS, window_extent // QS, QS)).reshape(element_tally, SSM_HEADS, window_extent)
    destination_places = jax.random.randint(jax.random.fold_in(diagonal_lookup_vector, 4), (element_tally, packet_clusters), 0, window_extent)
    struck = jnp.any(jnp.arange(window_extent)[None, None, :] == destination_places[:, :, None], axis=1)
    return base_rate * rough * block_factor + 0.32 * struck[:, None, :].astype(jnp.float32)


def draw_prompt_dt(key, part):
    return change_sizes_abs(key, jax.random.fold_in(key, 31), PROMPTS, PLEN, 2)


def draw_resp_dt(key, part):
    return change_sizes_abs(key, jax.random.fold_in(key, 32), RESPONSES, RLEN, 1)


def place_ends(entries, own_key, smallest, top_value):
    extent = entries.shape
    place = [jax.random.randint(jax.random.fold_in(own_key, axis), (), 0, extent[axis]) for axis in range(len(extent))]
    entries = entries.at[tuple(place)].set(smallest)
    longest = extent.index(max(extent))
    place[longest] = (place[longest] + 1) % extent[longest]
    return entries.at[tuple(place)].set(top_value)


def levels(stream_key, extent, pieces, low, largest):
    gain = 1.0
    for dim, blocks in pieces:
        heights = jax.random.uniform(jax.random.fold_in(jax.random.fold_in(stream_key, 6), dim), (blocks,), jnp.float32, low / len(pieces), largest / len(pieces))
        gain = gain * jnp.repeat(jnp.exp(heights), extent[dim] // blocks).reshape((-1,) + (1,) * (len(extent) - 1 - dim))
    return gain


def profile(count, total, bound, lean):
    portions = [(1 << 20) // math.isqrt(grade ** lean) + 1 for grade in range(2, count + 1)]
    spare, counts = total - bound - (count - 1), [1] * (count - 1)
    while spare > 0:
        candidates = [i for i in range(count - 1) if counts[i] < bound]
        mass, budget = sum([portions[i] for i in candidates]), spare
        for i in candidates:
            addition = min(bound - counts[i], max(1, budget * portions[i] // mass), spare)
            counts[i] = counts[i] + addition
            spare = spare - addition
    return np.array([bound] + counts)


def uneven_parts(rng, amount, total, reach, lean):
    if amount == 2:
        one = jax.random.randint(rng, (), max(1, total - reach), min(reach, total - 1) + 1)
        return jnp.stack([one, total - one])
    lengths = jnp.asarray(profile(amount, total, reach, lean), jnp.int32)
    twos = (amount - 1) // 2
    donor, receiver = lengths[1:1 + 2 * twos:2], lengths[2:2 + 2 * twos:2]
    room = jnp.minimum(donor - 1, reach - receiver)
    moved = jax.random.randint(jax.random.fold_in(rng, 1), (twos,), 0, 1 << 20) % (room + 1)
    lengths = lengths.at[1:1 + 2 * twos:2].set(donor - moved).at[2:2 + 2 * twos:2].set(receiver + moved)
    return lengths[jax.random.permutation(jax.random.fold_in(rng, 2), amount)]


def normal_values(rng, dims, scale, reach, cuts=(), held_as=jnp.bfloat16):
    drawn = jax.random.normal(rng, dims, jnp.float32) * scale
    if len(cuts) > 0:
        drawn = levels(rng, dims, cuts, -0.22, 0.18) * drawn
    return jnp.clip(drawn, min=-reach, max=reach).astype(held_as)


def setup_inputs(seed: int = 0) -> dict:
    key_list = jax.random.split(jax.random.key(seed), 17)
    return {
        "prompt_keys": draw_prompt_keys(jax.random.fold_in(key_list[16], 71), 0),
        "prompt_values": normal_values(key_list[1], (PROMPTS, PLEN, KVH * HDIM), 1.0, 6.0, ((1, 8),)),
        "resp_query": draw_resp_query(jax.random.fold_in(key_list[16], 71), 0),
        "resp_keys": normal_values(key_list[3], (RESPONSES, RLEN, KVH * HDIM), 1.0, 6.0, ((0, 4),)),
        "resp_values": normal_values(key_list[4], (RESPONSES, RLEN, KVH * HDIM), 1.0, 6.0, ((0, 4),)),
        "prompt_x": draw_prompt_x(jax.random.fold_in(key_list[16], 71), 0),
        "prompt_dt": draw_prompt_dt(jax.random.fold_in(key_list[16], 71), 0),
        "prompt_b": normal_values(key_list[7], (PROMPTS, PLEN, NST), 1.0, 6.0, ((1, 8),)),
        "prompt_c": normal_values(key_list[8], (PROMPTS, PLEN, NST), NST ** -0.5, 0.5, ((1, 8),)),
        "resp_x": normal_values(key_list[9], (RESPONSES, RLEN, SSM_HEADS * SP), 1.0, 6.0, ((0, 4), (2, 8))),
        "resp_dt": draw_resp_dt(jax.random.fold_in(key_list[16], 71), 0),
        "resp_b": normal_values(key_list[11], (RESPONSES, RLEN, NST), 1.0, 6.0, ((0, 4),)),
        "resp_c": normal_values(key_list[12], (RESPONSES, RLEN, NST), NST ** -0.5, 0.5, ((0, 4),)),
        "ssm_rate": jnp.clip(jnp.exp(jax.random.uniform(key_list[13], (SSM_HEADS,), jnp.float32, math.log(0.7), math.log(1.4))), 0.7, 1.4),
        "resp_group": place_ends(jax.random.randint(key_list[14], (RESPONSES,), 0, PROMPTS), jax.random.fold_in(key_list[14], 1), 0, PROMPTS - 1).astype(jnp.int32),
        "resp_len": uneven_parts(key_list[15], RESPONSES, RESPONSES * RLEN * 5 // 8, RLEN, 1).astype(jnp.int32),
    }


EPS = 1e-05

def block_ref(inputs, steps, b_rows, c_rows, rates, state):
    exponent = jnp.cumsum(-steps * rates[:, None], axis=1)
    width = inputs.shape[0]
    lower = jnp.arange(width)[:, None] >= jnp.arange(width)[None, :]
    spread = jnp.where(lower[None], exponent[:, :, None] - exponent[:, None, :], -jnp.inf)
    gram = jnp.dot(c_rows, b_rows.T, preferred_element_type=jnp.float32)
    mixing = (jnp.exp(spread) * gram[None] * steps[:, None, :]).astype(jnp.bfloat16)
    local = jnp.einsum('hts,shp->thp', mixing.astype(jnp.float32), inputs.astype(jnp.float32))
    carried = jnp.einsum('tn,hpn->thp', c_rows.astype(jnp.float32), state, precision=lax.Precision.HIGHEST)
    output = local + carried * jnp.exp(exponent).T[:, :, None]
    last = exponent[:, -1]
    weighted = (inputs.astype(jnp.float32) * (jnp.exp(last[:, None] - exponent) * steps).T[:, :, None]).astype(jnp.bfloat16)
    fresh = jnp.einsum('thp,tn->hpn', weighted.astype(jnp.float32), b_rows.astype(jnp.float32))
    return (output, jnp.exp(last)[:, None, None] * state + fresh)

def sequence_ref(inputs, steps, b_rows, c_rows, rates, state):
    window_extent = inputs.shape[0]
    heads = steps.shape[0]
    blocks = window_extent // QS
    xs = inputs.reshape(blocks, QS, heads, SP)
    ss = steps.reshape(heads, blocks, QS).transpose(1, 0, 2)
    bs = b_rows.reshape(blocks, QS, NST)
    cs = c_rows.reshape(blocks, QS, NST)

    def advance(carry, block):
        out, carry_next = block_ref(block[0], block[1], block[2], block[3], rates, carry)
        return (carry_next, out)
    final, outs = lax.scan(advance, state, (xs, ss, bs, cs))
    return (outs.reshape(window_extent, heads, SP), final)

def head_norm(values):
    scale = lax.rsqrt(lax.optimization_barrier(jnp.mean(values * values, axis=-1, keepdims=True)) + EPS)
    return (values * scale).reshape(values.shape[0], -1)

def reference(prompt_keys, prompt_values, resp_query, resp_keys, resp_values, prompt_x, prompt_dt, prompt_b, prompt_c, resp_x, resp_dt, resp_b, resp_c, ssm_rate, resp_group, resp_len):
    prompt_outs = []
    finals = []
    for prompt in range(PROMPTS):
        out, final = sequence_ref(prompt_x[prompt], prompt_dt[prompt], prompt_b[prompt], prompt_c[prompt], ssm_rate, jnp.zeros((SSM_HEADS, SP, NST), jnp.float32))
        prompt_outs.append(head_norm(out).astype(jnp.bfloat16))
        finals.append(final)
    prompt_ssm_out = jnp.stack(prompt_outs)
    finals = jnp.stack(finals)

    def one_state(items):
        inputs, steps, b_rows, c_rows, group, window_extent = items
        start = lax.dynamic_index_in_dim(finals, group.astype(jnp.int32), 0, keepdims=False)
        out, final = sequence_ref(inputs, steps, b_rows, c_rows, ssm_rate, start)
        valid = jnp.arange(RLEN) < window_extent
        return jnp.where(valid[:, None], head_norm(out), 0.0).astype(jnp.bfloat16)
    resp_ssm_out = lax.map(one_state, (resp_x, resp_dt, resp_b, resp_c, resp_group, resp_len))
    scale = 1.0 / HDIM ** 0.5

    def one_attention(items):
        queries, own_keys, own_values, group, window_extent = items
        group = group.astype(jnp.int32)
        key_rows = jnp.concatenate([lax.dynamic_index_in_dim(prompt_keys, group, 0, keepdims=False), own_keys], axis=0)
        value_rows = jnp.concatenate([lax.dynamic_index_in_dim(prompt_values, group, 0, keepdims=False), own_values], axis=0)
        element_tally = PLEN + RLEN
        key_rows = key_rows.reshape(element_tally, KVH, HDIM).transpose(1, 0, 2)
        value_rows = value_rows.reshape(element_tally, KVH, HDIM).transpose(1, 0, 2)
        grouped = queries.reshape(RLEN, KVH, QPK, HDIM).transpose(1, 0, 2, 3)
        position = jnp.arange(RLEN)
        column = jnp.arange(element_tally)
        allowed = (column[None, :] < PLEN) | (column[None, :] - PLEN <= position[:, None])
        valid = position < window_extent

        def per_head(parts):
            head_queries, head_keys, head_values = parts
            score = jnp.einsum('tqd,sd->tqs', head_queries.astype(jnp.float32), head_keys.astype(jnp.float32)) * scale
            score = jnp.where(allowed[:, None, :], score, -jnp.inf)
            top = lax.optimization_barrier(jnp.max(score, axis=-1, keepdims=True))
            raised = jnp.exp(score - top)
            total = lax.optimization_barrier(jnp.sum(raised, axis=-1, keepdims=True))
            weights = raised.astype(jnp.bfloat16)
            mixed = jnp.einsum('tqs,sd->tqd', weights.astype(jnp.float32), head_values.astype(jnp.float32)) / total
            return jnp.where(valid[:, None, None], mixed, 0.0).astype(jnp.bfloat16)
        result = lax.map(per_head, (grouped, key_rows, value_rows))
        return result.transpose(1, 0, 2, 3).reshape(RLEN, HEADS * HDIM)
    resp_attn_out = lax.map(one_attention, (resp_query, resp_keys, resp_values, resp_group, resp_len))
    return (resp_attn_out, resp_ssm_out, prompt_ssm_out)
```

```python
import functools
import math

import jax
import jax.numpy as jnp
from jax import lax
from jax.experimental import pallas as pl
from jax.experimental.pallas import tpu as pltpu
from jax.sharding import PartitionSpec as P

HDIM = 128
SP = 64
NST = 128
QS = 128
EPS = 1e-05
LANES = 128
VMEM_LIMIT = 48 * 1024 * 1024


def ssm_kernel(
    group_ref, len_ref, x_ref, dt_ref, b_ref, c_ref, rate_ref, *refs, heads, sub, from_start
):
    if from_start:
        start_ref, out_ref, state_ref = refs
        final_ref = None
    else:
        out_ref, final_ref, state_ref = refs
    item = pl.program_id(0)
    step = pl.program_id(1)
    length = len_ref[item]

    @pl.when(step == 0)
    def _():
        if from_start:
            state_ref[...] = start_ref[0]
        else:
            state_ref[...] = jnp.zeros_like(state_ref)

    rows = lax.broadcasted_iota(jnp.int32, (QS, QS), 0)
    cols = lax.broadcasted_iota(jnp.int32, (QS, QS), 1)
    first_half = cols < SP

    def one_block(index):
        span = slice(index * QS, (index + 1) * QS)
        steps = dt_ref[0, :, span]
        upto = (rows <= cols).astype(jnp.float32)
        decay = lax.dot_general(
            steps * -rate_ref[...],
            upto,
            (((1,), (0,)), ((), ())),
            precision=lax.Precision.HIGHEST,
            preferred_element_type=jnp.float32,
        )
        decay_col = decay.T
        scale_col = jnp.exp(decay_col)
        weight_col = (jnp.exp(decay[:, QS - 1 :] - decay) * steps).T
        b_rows = b_ref[0, span, :]
        c_rows = c_ref[0, span, :]
        gram = lax.dot_general(
            c_rows, b_rows, (((1,), (1,)), ((), ())), preferred_element_type=jnp.float32
        )
        gram = jnp.where(rows >= cols, gram, 0.0)
        state = state_ref[...]
        coarse = state.astype(jnp.bfloat16)
        fine = (state - coarse.astype(jnp.float32)).astype(jnp.bfloat16)
        carried = jnp.dot(
            jnp.concatenate([c_rows, c_rows], axis=1),
            jnp.concatenate([coarse, fine], axis=0),
            preferred_element_type=jnp.float32,
        )
        same_head = ((rows < SP) == first_half).astype(jnp.bfloat16)
        position = step * (sub * QS) + index * QS + rows
        weighted = []
        kept = []
        for pair in range(heads // 2):
            lanes = slice(pair * LANES, (pair + 1) * LANES)
            x_pair = x_ref[0, span, lanes]
            mixes = []
            for head in (2 * pair, 2 * pair + 1):
                spread = decay_col[:, head : head + 1] - decay[head : head + 1, :]
                mix = jnp.exp(jnp.minimum(spread, 0.0)) * (gram * steps[head : head + 1, :])
                mixes.append(mix.astype(jnp.bfloat16))
            zero = jnp.zeros_like(x_pair)
            apart = jnp.concatenate(
                [jnp.where(first_half, x_pair, zero), jnp.where(first_half, zero, x_pair)], axis=0
            )
            local = jnp.dot(
                jnp.concatenate(mixes, axis=1), apart, preferred_element_type=jnp.float32
            )
            low, high = slice(2 * pair, 2 * pair + 1), slice(2 * pair + 1, 2 * pair + 2)
            scale = jnp.where(first_half, scale_col[:, low], scale_col[:, high])
            y = local + scale * carried[:, lanes]
            squares = jnp.dot(
                (y * y).astype(jnp.bfloat16), same_head, preferred_element_type=jnp.float32
            )
            out = y * lax.rsqrt(squares * (1.0 / SP) + EPS)
            if from_start:
                out = jnp.where(position < length, out, 0.0)
            out_ref[0, span, lanes] = out.astype(jnp.bfloat16)
            weight = jnp.where(first_half, weight_col[:, low], weight_col[:, high])
            weighted.append((weight * x_pair.astype(jnp.float32)).astype(jnp.bfloat16))
            kept.append(scale[QS - 1 :, :])
        fresh = lax.dot_general(
            b_rows,
            jnp.concatenate(weighted, axis=1),
            (((0,), (0,)), ((), ())),
            preferred_element_type=jnp.float32,
        )
        state_ref[...] = jnp.concatenate(kept, axis=1) * state + fresh

    if from_start:
        live = step * (sub * QS) < length

        @pl.when(live)
        def _():
            for index in range(sub):
                one_block(index)

        @pl.when(jnp.logical_not(live))
        def _():
            out_ref[...] = jnp.zeros_like(out_ref)
    else:
        for index in range(sub):
            one_block(index)

        @pl.when(step == pl.num_programs(1) - 1)
        def _():
            final_ref[0] = state_ref[...]


def ssm_call(x, dt, b_rows, c_rows, rates, group, length, start=None, sub=2, columns=(0, 0)):
    items, slots, width = x.shape
    heads = dt.shape[1]
    rows = sub * QS
    from_start = start is not None
    in_specs = [
        pl.BlockSpec((1, rows, width), lambda i, j, g, n: (i, j, 0)),
        pl.BlockSpec((1, heads, rows), lambda i, j, g, n: (i, 0, j)),
        pl.BlockSpec((1, rows, NST), lambda i, j, g, n: (i, j, columns[0])),
        pl.BlockSpec((1, rows, NST), lambda i, j, g, n: (i, j, columns[1])),
        pl.BlockSpec((heads, 1), lambda i, j, g, n: (0, 0)),
    ]
    out_specs = [pl.BlockSpec((1, rows, width), lambda i, j, g, n: (i, j, 0))]
    out_shape = [jax.ShapeDtypeStruct((items, slots, width), jnp.bfloat16)]
    args = [x, dt, b_rows, c_rows, rates[:, None]]
    if from_start:
        in_specs.append(pl.BlockSpec((1, NST, width), lambda i, j, g, n: (g[i], 0, 0)))
        args.append(start)
    else:
        out_specs.append(pl.BlockSpec((1, NST, width), lambda i, j, g, n: (i, 0, 0)))
        out_shape.append(jax.ShapeDtypeStruct((items, NST, width), jnp.float32))
    units = items * (slots // QS) * heads
    return pl.pallas_call(
        functools.partial(ssm_kernel, heads=heads, sub=sub, from_start=from_start),
        grid_spec=pltpu.PrefetchScalarGridSpec(
            num_scalar_prefetch=2,
            grid=(items, slots // rows),
            in_specs=in_specs,
            out_specs=out_specs,
            scratch_shapes=[pltpu.VMEM((NST, width), jnp.float32)],
        ),
        out_shape=out_shape,
        compiler_params=pltpu.CompilerParams(
            dimension_semantics=("arbitrary", "arbitrary"), vmem_limit_bytes=VMEM_LIMIT
        ),
        cost_estimate=pl.CostEstimate(
            flops=units * QS * QS * SP * 8,
            bytes_accessed=4 * items * slots * width,
            transcendentals=units * QS * QS,
        ),
        name="ssm_resp" if from_start else "ssm_prompt",
    )(group, length, *args)


def attn_kernel(
    group_ref, len_ref, own_ref, q_ref, pk_ref, pv_ref, rk_ref, rv_ref, out_ref, *, block, heads
):
    item = pl.program_id(0)
    turn = pl.program_id(1)
    length = len_ref[item]
    slots = rk_ref.shape[1]
    factor = math.log2(math.e) / math.sqrt(HDIM)
    rows = lax.broadcasted_iota(jnp.int32, (block, block), 0)
    cols = lax.broadcasted_iota(jnp.int32, (block, block), 1)

    def with_ones(values):
        return jnp.concatenate([values, jnp.ones_like(values)], axis=1)

    def score(queries, keys):
        return lax.dot_general(
            queries, keys, (((1,), (1,)), ((), ())), preferred_element_type=jnp.float32
        )

    for now in range(slots // block):

        @pl.when((turn == now) & (now * block < length))
        def _():
            valid = now * block + lax.broadcasted_iota(jnp.int32, (block, 1), 0) < length
            for head in range(heads):
                lanes = slice(head * HDIM, (head + 1) * HDIM)
                queries = q_ref[0, :, lanes]
                parts = [(score(queries, pk_ref[0]), pv_ref[0])]
                if now:
                    past = slice(0, now * block)
                    parts.append((score(queries, rk_ref[0, past, :]), rv_ref[0, past, :]))
                here = slice(now * block, (now + 1) * block)
                edge = jnp.where(rows >= cols, score(queries, rk_ref[0, here, :]), -jnp.inf)
                parts.append((edge, rv_ref[0, here, :]))
                top = functools.reduce(
                    jnp.maximum, [jnp.max(s, axis=1, keepdims=True) for s, _ in parts]
                )
                total = 0.0
                for s, values in parts:
                    weights = jnp.exp2((s - top) * factor).astype(jnp.bfloat16)
                    total = total + jnp.dot(
                        weights, with_ones(values), preferred_element_type=jnp.float32
                    )
                mixed = total[:, :HDIM] / total[:, HDIM:]
                out_ref[0, :, lanes] = jnp.where(valid, mixed, 0.0).astype(jnp.bfloat16)

    @pl.when(turn * block >= length)
    def _():
        out_ref[...] = jnp.zeros_like(out_ref)


def attn_call(queries, prompt_kv, resp_keys, resp_values, group, length, own, block=256):
    items, slots, width = queries.shape
    prompts = prompt_kv.shape[0] // 2
    prompt_len = prompt_kv.shape[1]
    q_spec = pl.BlockSpec((1, block, width), lambda i, j, g, n, o: (i, j, 0))
    own_spec = pl.BlockSpec((1, slots, HDIM), lambda i, j, g, n, o: (i, 0, o[0]))
    return pl.pallas_call(
        functools.partial(attn_kernel, block=block, heads=width // HDIM),
        grid_spec=pltpu.PrefetchScalarGridSpec(
            num_scalar_prefetch=3,
            grid=(items, slots // block),
            in_specs=[
                q_spec,
                pl.BlockSpec((1, prompt_len, HDIM), lambda i, j, g, n, o: (g[i], 0, 0)),
                pl.BlockSpec((1, prompt_len, HDIM), lambda i, j, g, n, o: (prompts + g[i], 0, 0)),
                own_spec,
                own_spec,
            ],
            out_specs=q_spec,
        ),
        out_shape=jax.ShapeDtypeStruct(queries.shape, jnp.bfloat16),
        compiler_params=pltpu.CompilerParams(
            dimension_semantics=("arbitrary", "arbitrary"), vmem_limit_bytes=VMEM_LIMIT
        ),
        cost_estimate=pl.CostEstimate(
            flops=4 * items * slots * width * (prompt_len + slots // 2),
            bytes_accessed=4 * items * slots * width,
            transcendentals=items * slots * (width // HDIM) * (prompt_len + slots // 2),
        ),
        name="attn",
    )(group, length, own, queries, prompt_kv, prompt_kv, resp_keys, resp_values)


def body(
    prompt_keys,
    prompt_values,
    resp_query,
    resp_keys,
    resp_values,
    prompt_x,
    prompt_dt,
    prompt_b,
    prompt_c,
    resp_x,
    resp_dt,
    resp_b,
    resp_c,
    ssm_rate,
    resp_group,
    resp_len,
):
    seq_index = lax.axis_index("seq")
    resp_index = lax.axis_index("resp")
    seq_count = lax.axis_size("seq")
    resp_count = lax.axis_size("resp")
    prompt_count, shard_rows, _ = prompt_x.shape
    prompt_heads = prompt_dt.shape[1]
    resp_heads = resp_dt.shape[1]
    key_heads = prompt_keys.shape[2] // HDIM
    repeat = seq_count // key_heads

    moved_x = lax.all_to_all(prompt_x, "seq", split_axis=2, concat_axis=1, tiled=True)
    moved_dt = lax.all_to_all(prompt_dt, "seq", split_axis=1, concat_axis=2, tiled=True)
    moved_bc = lax.all_gather(
        jnp.concatenate([prompt_b, prompt_c], axis=2), "seq", axis=1, tiled=True
    )
    kv = jnp.concatenate([prompt_keys, prompt_values], axis=0)
    kv = jnp.repeat(kv.reshape(2 * prompt_count, shard_rows, key_heads, HDIM), repeat, axis=2)
    kv = kv.reshape(2 * prompt_count, shard_rows, seq_count * HDIM)
    moved_kv = lax.all_to_all(kv, "seq", split_axis=2, concat_axis=1, tiled=True)

    scan_heads = prompt_heads // seq_count
    scan_rates = lax.dynamic_slice_in_dim(
        ssm_rate, resp_index * prompt_heads + seq_index * scan_heads, scan_heads
    )
    none = jnp.zeros((prompt_count,), jnp.int32)
    scanned, finals = ssm_call(
        moved_x, moved_dt, moved_bc, moved_bc, scan_rates, none, none, columns=(0, 1)
    )
    prompt_ssm_out = lax.all_to_all(scanned, "seq", split_axis=1, concat_axis=2, tiled=True)

    route = []
    for s in range(seq_count):
        for r in range(resp_count):
            piece = r * seq_count + s
            route.append((s * resp_count + r, piece))
    piece = lax.ppermute(finals, ("seq", "resp"), route)
    start = lax.all_gather(piece, "resp", axis=2, tiled=True)

    own = (seq_index // repeat).astype(jnp.int32)[None]
    resp_attn_out = attn_call(
        resp_query, moved_kv, resp_keys, resp_values, resp_group, resp_len, own
    )
    resp_rates = lax.dynamic_slice_in_dim(ssm_rate, seq_index * resp_heads, resp_heads)
    (resp_ssm_out,) = ssm_call(
        resp_x, resp_dt, resp_b, resp_c, resp_rates, resp_group, resp_len, start
    )
    return (resp_attn_out, resp_ssm_out, prompt_ssm_out)


def solution(mesh):
    placed = (
        P(None, "seq", None),
        P(None, "seq", None),
        P("resp", None, "seq"),
        P("resp", None, None),
        P("resp", None, None),
        P(None, "seq", "resp"),
        P(None, "resp", "seq"),
        P(None, "seq", None),
        P(None, "seq", None),
        P("resp", None, "seq"),
        P("resp", "seq", None),
        P("resp", None, None),
        P("resp", None, None),
        P(),
        P("resp"),
        P("resp"),
    )
    return jax.shard_map(
        body,
        mesh=mesh,
        in_specs=placed,
        out_specs=(P("resp", None, "seq"), P("resp", None, "seq"), P(None, "seq", "resp")),
        check_vma=False,
    )
```
